32 devices in a mesh: dp: 4 (over x, core), expert: 8 (over z, y).
Axes of the slice: x: 2, y: 2, z: 4, core: 2. Of those that a mesh axis runs over, the one named last changes fastest.
Arguments:
- tokens: bfloat16 [8192, 3584], P(('dp', 'expert')), may hold values from -6 to 6
- cotangent: bfloat16 [8192, 3584], P(('dp', 'expert')), may hold values from -0.59765625 to 0.59765625
- expert_ids: int32 [8192, 1], P(('dp', 'expert')), may hold values from 0 to 7; in each aligned block of 256 rows (0 to 255, 256 to 511, ...) at most 48 rows name the same one
- gates: float32 [8192, 1], P(('dp', 'expert')), may hold values from 0.2 to 1
- pair_flags: int32 [8], replicated, may hold values from 0 to 1, as said below
- w_in: bfloat16 [8, 3584, 1024], P('expert', None, 'dp'), may hold values from -0.09375 to 0.09375
- w_out: bfloat16 [8, 1024, 3584], P('expert', 'dp'), may hold values from -0.1875 to 0.1875
Outputs:
- mixed: bfloat16 [8192, 3584], P(('dp', 'expert'))
- grad_in: bfloat16 [8, 3584, 1024], P('expert', None, 'dp')
- grad_out: bfloat16 [8, 1024, 3584], P('expert', 'dp')
The draws below stay inside these ranges and needn't reach their ends.
Inputs may be any that keep to these rules, and one draw needn't show every extreme that they name: `expert_ids`: among the 256 tokens of one device, no expert is named by more than 48 routes; some expert is named exactly 48 times. pair_flags[j] equals pair_flags[j XOR (4)].
All inputs are finite; a program needn't handle non-finite values.
Results may differ from the reference program's by a relative error of at most 0.015.
Values may be sent and summed in bfloat16 or wider, within the bound.
A program may use at most 192 MiB of HBM per device.

```python
import math
import jax
import jax.numpy as jnp
import numpy as np
from jax import lax

D = 3584
H = 1024
TOK_DEV = 256
TOP = 1
EXPERTS = 8
C = 48
TOKENS = 8192
N_DP = 4


def draw_pair_flags(key, part):
    half_count = EXPERTS // 2
    key_bits = jax.random.fold_in(key, 11)
    key_one = jax.random.fold_in(key, 12)
    key_gap = jax.random.fold_in(key, 13)
    base = jax.random.randint(key_bits, (half_count,), 0, 2, dtype=jnp.int32)
    first_lane = jax.random.randint(key_one, (), 0, half_count, dtype=jnp.int32)
    gap_lane = jax.random.randint(key_gap, (), 1, half_count, dtype=jnp.int32)
    second_lane = ((first_lane + gap_lane) % half_count).astype(jnp.int32)
    lanes = jnp.arange(half_count, dtype=jnp.int32)
    base = jnp.where(lanes == first_lane, 1, jnp.where(lanes == second_lane, 0, base)).astype(jnp.int32)
    return jnp.concatenate([base, base]).astype(jnp.int32)


def levels(own_key, dims, split, least, largest):
    factor_of, own = 1.0, jax.random.fold_in(own_key, 6)
    for axis_at, blocks in split:
        heights = jnp.exp(jax.random.uniform(jax.random.fold_in(own, axis_at), (blocks,), jnp.float32, least / len(split), largest / len(split)))
        factor_of = factor_of * jnp.repeat(heights, dims[axis_at] // blocks).reshape([-1 if axis == axis_at else 1 for axis in range(len(dims))])
    return factor_of


def assign_block(key, own, number, rows, amount, top, most, slope):
    ranking = jax.random.permutation(key, amount)
    heavy_load, usual = load_shares(amount, rows * top, most, slope, True), load_shares(amount, rows * top, most, slope, False)
    places = jnp.arange(amount)

    def named(lengths, rotation):
        used = int((lengths > 0).sum())
        fixed = max(1, used // 4)
        passed = fixed + (places - fixed + rotation * (used - fixed)) % max(1, amount - fixed)
        return jnp.zeros((amount,), jnp.int32).at[ranking[jnp.where(places < fixed, places, passed)]].set(jnp.asarray(lengths, jnp.int32))

    lengths = jnp.where(number % 4 == 0, named(heavy_load, number // 4), named(usual, number - number // 4 - 1))
    mixed = jax.random.permutation(jax.random.fold_in(own, 3), amount)
    giver, sink = mixed[0:amount // 2 * 2:2], mixed[1:amount // 2 * 2:2]
    slack = jnp.minimum(lengths[giver] - 1, most - lengths[sink]) // 2
    slack = jnp.where((giver == ranking[0]) | (sink == ranking[0]) | (lengths[sink] == 0), 0, jnp.maximum(slack, 0))
    passed = jax.random.randint(jax.random.fold_in(own, 4), (amount // 2,), 0, 1 << 20) % (slack + 1)
    lengths = lengths.at[giver].add(-passed).at[sink].add(passed)
    members = jnp.searchsorted(jnp.cumsum(lengths), jnp.arange(rows * top), side="right").astype(jnp.int32)
    listing = members.reshape(top, rows).T
    listing = listing[jax.random.permutation(jax.random.fold_in(own, 1), rows)]
    rotation = jax.random.randint(jax.random.fold_in(own, 2), (rows, 1), 0, top)
    return jnp.take_along_axis(listing, (jnp.arange(top)[None, :] + rotation) % top, axis=1)


def load_shares(count, total, bound, skew, full):
    weights = [(1 << 20) // math.isqrt(grade ** skew) + 1 for grade in range(1, count + 1)]
    largest = bound if full else min(bound, max(-(-total // count), total * weights[0] // sum(weights)))
    least = 1 if total - largest >= count - 1 else 0
    holding, spare = [largest] + [least] * (count - 1), total - largest - least * (count - 1)
    while spare > 0:
        free = [i for i in range(1, count) if holding[i] < largest] or [i for i in range(1, count) if holding[i] < bound]
        whole, left = sum([weights[i] for i in free]), spare
        for i in free:
            extra = min(bound - holding[i], max(1, left * weights[i] // whole), spare)
            holding[i] = holding[i] + extra
            spare = spare - extra
    return np.array(holding)


def bell_draw(stream_key, extent, width, most, shards=(), held_as=jnp.bfloat16):
    result = width * jax.random.normal(stream_key, extent, jnp.float32)
    if shards:
        result = result * levels(stream_key, extent, shards, -0.22, 0.18)
    return jnp.clip(result, -most, most).astype(held_as)


def setup_inputs(seed: int = 0) -> dict:
    keys = jax.random.split(jax.random.key(seed), 8)
    tokens = bell_draw(keys[0], (TOKENS, D), 1.0, 6.0, ((0, 32),))
    cotangent = bell_draw(keys[1], (TOKENS, D), 0.1, 0.59765625, ((0, 32),))
    expert_ids_keys = jax.random.split(jax.random.fold_in(keys[2], 1), TOKENS // TOK_DEV)
    expert_ids_turns = jax.random.permutation(jax.random.fold_in(keys[2], 3), TOKENS // TOK_DEV)
    expert_ids = jax.vmap(lambda own, number: assign_block(jax.random.fold_in(keys[2], 2), own, number, TOK_DEV, EXPERTS, TOP, C, 2))(expert_ids_keys, expert_ids_turns).reshape((TOKENS, TOP))
    gates = jnp.clip(0.2 + 0.8 * jax.random.uniform(keys[3], (TOKENS, TOP), jnp.float32) ** levels(keys[3], (TOKENS, TOP), ((0, 32),), -0.2, 0.2), 0.2, 1.0)
    pair_flags = draw_pair_flags(jax.random.fold_in(keys[7], 71), 0)
    w_in = bell_draw(keys[5], (EXPERTS, D, H), D ** -0.5, 0.09375, ((0, 8), (2, 4)))
    w_out = bell_draw(keys[6], (EXPERTS, H, D), H ** -0.5, 0.1875, ((0, 8), (1, 4)))
    return dict(tokens=tokens, cotangent=cotangent, expert_ids=expert_ids, gates=gates, pair_flags=pair_flags, w_in=w_in, w_out=w_out)


def reference(tokens, cotangent, expert_ids, gates, pair_flags, w_in, w_out):
    routed_count = TOKENS * TOP
    ids = expert_ids.reshape(-1).astype(jnp.int32)
    token_of = (jnp.arange(routed_count) // TOP).astype(jnp.int32)
    replica = (token_of // (TOK_DEV * EXPERTS)).astype(jnp.int32)
    weight = gates.reshape(-1)
    scaled = (weight[:, None] * cotangent[token_of].astype(jnp.float32)).astype(jnp.bfloat16)
    scaled_ext = jnp.concatenate([scaled, jnp.zeros((1, D), jnp.bfloat16)], axis=0)
    tokens_ext = jnp.concatenate([tokens, jnp.zeros((1, D), jnp.bfloat16)], axis=0)
    token_ext = jnp.concatenate([token_of, jnp.full((1,), TOKENS, jnp.int32)]).astype(jnp.int32)
    group = (ids * N_DP + replica).astype(jnp.int32)
    order = jnp.argsort(group, stable=True).astype(jnp.int32)
    counts = jnp.sum((group[:, None] == jnp.arange(EXPERTS * N_DP, dtype=jnp.int32)[None, :]).astype(jnp.int32), axis=0).astype(jnp.int32)
    starts = (jnp.cumsum(counts) - counts).astype(jnp.int32)
    span = EXPERTS * C
    order_ext = jnp.concatenate([order, jnp.full((span,), routed_count, jnp.int32)]).astype(jnp.int32)
    lanes = jnp.arange(span, dtype=jnp.int32)

    def step(carry, expert):
        win = w_in[expert]
        wout = w_out[expert]
        sum_in = jnp.zeros((D, H), jnp.float32)
        sum_out = jnp.zeros((H, D), jnp.float32)
        for rep in range(N_DP):
            slot = expert * N_DP + rep
            index = lax.dynamic_slice_in_dim(order_ext, starts[slot], span)
            index = jnp.where(lanes < counts[slot], index, routed_count).astype(jnp.int32)
            xrows = tokens_ext[token_ext[index]]
            drows = scaled_ext[index]
            pre = jnp.dot(xrows, win, preferred_element_type=jnp.float32)
            sig = jax.nn.sigmoid(pre)
            hidden = (pre * sig).astype(jnp.bfloat16)
            out_rows = jnp.dot(hidden, wout, preferred_element_type=jnp.float32).astype(jnp.bfloat16)
            carry = carry.at[index].set(out_rows, mode="drop")
            dhid = jnp.dot(drows, wout.T, preferred_element_type=jnp.float32)
            dpre = (dhid * sig * (1.0 + pre * (1.0 - sig))).astype(jnp.bfloat16)
            part_out = lax.optimization_barrier(jnp.dot(hidden.T, drows, preferred_element_type=jnp.float32).astype(jnp.bfloat16))
            part_in = lax.optimization_barrier(jnp.dot(xrows.T, dpre, preferred_element_type=jnp.float32).astype(jnp.bfloat16))
            sum_out = sum_out + part_out.astype(jnp.float32)
            sum_in = sum_in + part_in.astype(jnp.float32)
        return carry, (sum_in.astype(jnp.bfloat16), sum_out.astype(jnp.bfloat16))

    outs, grads = lax.scan(step, jnp.zeros((routed_count, D), jnp.bfloat16), jnp.arange(EXPERTS, dtype=jnp.int32))
    full_in, full_out = grads
    mixed = jnp.sum(weight.reshape(TOKENS, TOP, 1) * outs.reshape(TOKENS, TOP, D).astype(jnp.float32), axis=1).astype(jnp.bfloat16)
    partner = jnp.bitwise_xor(jnp.arange(EXPERTS, dtype=jnp.int32), (EXPERTS // 2) * pair_flags).astype(jnp.int32)
    return mixed, full_in[partner], full_out[partner]
```

```python
import functools

import jax
import jax.numpy as jnp
from jax import lax
from jax.experimental import pallas as pl
from jax.experimental.pallas import tpu as pltpu
from jax.sharding import PartitionSpec as P

MESH = pl.DeviceIdType.MESH
F32 = jnp.float32
BF16 = jnp.bfloat16


def remote(src, dst, send, recv, target):
    copy = pltpu.make_async_remote_copy(
        src_ref=src,
        dst_ref=dst,
        send_sem=send,
        recv_sem=recv,
        device_id=target,
        device_id_type=MESH,
    )
    copy.start()
    return copy


def places(count):
    dp, me = lax.axis_index("dp"), lax.axis_index("expert")
    sibling = (dp + 1 - 2 * lax.rem(dp, 2), me)
    across = (lax.rem(dp + 2, 4), me)
    ahead = [None] + [lax.rem(me + k, count) for k in range(1, count)]
    behind = [None] + [lax.rem(me + count - k, count) for k in range(1, count)]
    return dp, me, sibling, across, ahead, behind


def greet(dp, sibling, across, ahead):
    barrier = pltpu.get_barrier_semaphore()
    targets = [sibling, across] + [(dp, peer) for peer in ahead[1:]]
    for target in targets:
        pl.semaphore_signal(barrier, inc=1, device_id=target, device_id_type=MESH)
    pl.semaphore_wait(barrier, len(targets))


def dispatch_kernel(count, x_ref, s_ref, win_ref, wout_ref, rows, grads, win_other, wout_pair,
                    a_send, a_recv, f_send, f_recv, w_send, w_recv, local):
    dp, me, sibling, across, ahead, behind = places(count)
    greet(dp, sibling, across, ahead)
    held = [
        remote(win_ref, win_other, w_send.at[0], w_recv.at[0], across),
        remote(wout_ref, wout_pair.at[1], w_send.at[1], w_recv.at[1], across),
    ]
    own = [pltpu.make_async_copy(wout_ref, wout_pair.at[0], local.at[2])]
    sent = []
    for at, (source, landed) in enumerate(((x_ref, rows), (s_ref, grads))):
        sent.append([None] + [
            remote(source.at[ahead[k]], landed.at[0, me], a_send.at[at, k], a_recv.at[at, k],
                   (dp, ahead[k]))
            for k in range(1, count)
        ])
    for at, (source, landed) in enumerate(((x_ref, rows), (s_ref, grads))):
        own.append(pltpu.make_async_copy(source.at[me], landed.at[0, me], local.at[at]))
        held.append(
            remote(source.at[me], landed.at[1, me], f_send.at[at, 0], f_recv.at[at, 0], sibling)
        )
    for copy in own:
        copy.start()
    for at, landed in enumerate((rows, grads)):
        for k in range(1, count):
            sent[at][k].wait_recv()
            block = behind[k]
            held.append(
                remote(landed.at[0, block], landed.at[1, block], f_send.at[at, k],
                       f_recv.at[at, k], sibling)
            )
    for copy in own:
        copy.wait()
    for group in sent:
        for copy in group[1:]:
            copy.wait_send()
    for copy in held:
        copy.wait()


def dispatch(x_send, s_send, win, wout, count):
    blocks = (2,) + x_send.shape
    anywhere = pl.BlockSpec(memory_space=pl.ANY)
    dma = pltpu.SemaphoreType.DMA
    return pl.pallas_call(
        functools.partial(dispatch_kernel, count),
        out_shape=(
            jax.ShapeDtypeStruct(blocks, BF16),
            jax.ShapeDtypeStruct(blocks, BF16),
            jax.ShapeDtypeStruct(win.shape, BF16),
            jax.ShapeDtypeStruct((2,) + wout.shape, BF16),
        ),
        in_specs=[anywhere] * 4,
        out_specs=(anywhere,) * 4,
        scratch_shapes=[
            dma((2, count)), dma((2, count)), dma((2, count)), dma((2, count)),
            dma((2,)), dma((2,)), dma((3,)),
        ],
        compiler_params=pltpu.CompilerParams(collective_id=0, has_side_effects=True),
    )(x_send, s_send, win, wout)


def combine_kernel(count, part_ref, gin_ref, gout_ref, back, gin_recv, gout_recv,
                   mine, theirs, total, p_send, p_recv, g_send, g_recv, r_send, r_recv, local):
    dp, me, sibling, across, ahead, behind = places(count)
    greet(dp, sibling, across, ahead)
    order = ahead[1:] + [me]
    parts, own = [], []
    for at, block in enumerate(order):
        parts.append(
            remote(part_ref.at[1, block], theirs.at[block], p_send.at[at], p_recv.at[at], sibling)
        )
        own.append(pltpu.make_async_copy(part_ref.at[0, block], mine.at[block], local.at[at]))
        own[-1].start()
    shares = [
        remote(gin_ref, gin_recv, g_send.at[0], g_recv.at[0], across),
        remote(gout_ref, gout_recv, g_send.at[1], g_recv.at[1], across),
    ]
    sent = []
    for at, block in enumerate(order):
        own[at].wait()
        parts[at].wait_recv()
        total[block] = (mine[block].astype(F32) + theirs[block].astype(F32)).astype(BF16)
        if at < count - 1:
            sent.append(
                remote(total.at[block], back.at[me], r_send.at[at], r_recv.at[at], (dp, block))
            )
        else:
            last = pltpu.make_async_copy(total.at[block], back.at[me], local.at[count])
            last.start()
    last.wait()
    for copy in parts:
        copy.wait_send()
    for copy in sent + shares:
        copy.wait()


def combine(part, gin, gout, count):
    blocks = part.shape[1:]
    anywhere = pl.BlockSpec(memory_space=pl.ANY)
    dma = pltpu.SemaphoreType.DMA
    return pl.pallas_call(
        functools.partial(combine_kernel, count),
        out_shape=(
            jax.ShapeDtypeStruct(blocks, BF16),
            jax.ShapeDtypeStruct(gin.shape, BF16),
            jax.ShapeDtypeStruct(gout.shape, BF16),
        ),
        in_specs=[anywhere] * 3,
        out_specs=(anywhere,) * 3,
        scratch_shapes=[
            pltpu.VMEM(blocks, BF16), pltpu.VMEM(blocks, BF16), pltpu.VMEM(blocks, BF16),
            dma((count,)), dma((count,)), dma((2,)), dma((2,)),
            dma((count,)), dma((count,)), dma((count + 1,)),
        ],
        compiler_params=pltpu.CompilerParams(
            collective_id=1, has_side_effects=True, vmem_limit_bytes=40 * 1024 * 1024
        ),
    )(part, gin, gout)


def body(tokens, cotangent, expert_ids, gates, pair_flags, w_in, w_out):
    count = lax.axis_size("expert")
    me = lax.axis_index("expert")
    half = count // 2
    local_tokens, top = expert_ids.shape
    width = tokens.shape[1]
    routes = local_tokens * top
    capacity = -(-max(2, 3 * routes // (2 * count)) // 16) * 16
    slots = count * capacity
    quarter_in, quarter_out = w_in[0], w_out[0]
    quarter = quarter_in.shape[1]
    last = (((1,), (1,)), ((), ()))
    first = (((0,), (0,)), ((), ()))

    ids = expert_ids.reshape(-1)
    onehot = ids[:, None] == jnp.arange(count, dtype=jnp.int32)[None, :]
    at = jnp.arange(routes, dtype=jnp.int32)
    before = (at[None, :] < at[:, None]).astype(BF16)
    rank = jnp.dot(before, onehot.astype(BF16), preferred_element_type=F32)
    position = jnp.sum(jnp.where(onehot, rank, 0.0), axis=1).astype(jnp.int32)
    slot_of = ids * capacity + position
    pick = (jnp.arange(slots, dtype=jnp.int32)[:, None] == slot_of[None, :]).astype(BF16)
    scaled = (gates.reshape(local_tokens, top, 1) * cotangent[:, None, :].astype(F32)).astype(BF16)
    scaled = scaled.reshape(routes, width)
    copied = tokens if top == 1 else jnp.repeat(tokens, top, axis=0)
    x_send = jnp.dot(pick, copied, preferred_element_type=F32).astype(BF16)
    s_send = jnp.dot(pick, scaled, preferred_element_type=F32).astype(BF16)

    rows, grads, other_in, pair_out = dispatch(
        x_send.reshape(count, capacity, width), s_send.reshape(count, capacity, width),
        quarter_in, quarter_out, count,
    )
    rows, grads = rows.reshape(2 * slots, width), grads.reshape(2 * slots, width)
    both_out = pair_out.reshape(2 * quarter, width)
    pre = jnp.concatenate(
        [jnp.dot(rows, quarter_in, preferred_element_type=F32),
         jnp.dot(rows, other_in, preferred_element_type=F32)], axis=1)
    sig = jax.nn.sigmoid(pre)
    hidden = (pre * sig).astype(BF16)
    part = jnp.dot(hidden, both_out, preferred_element_type=F32).astype(BF16)
    dhid = lax.dot_general(grads, both_out, last, preferred_element_type=F32)
    dpre = (dhid * sig * (1.0 + pre * (1.0 - sig))).astype(BF16)
    send_in = lax.dot_general(rows, dpre[:, quarter:], first, preferred_element_type=F32)
    send_out = lax.dot_general(hidden[:, quarter:], grads, first, preferred_element_type=F32)
    back, recv_in, recv_out = combine(
        part.reshape(2, count, capacity, width), send_in.astype(BF16), send_out.astype(BF16), count
    )

    groups = min(4, half)
    chosen = pair_flags[:half].reshape(half // groups, groups).max(axis=0)
    which = jnp.sum(chosen << jnp.arange(groups, dtype=jnp.int32))
    flagged = pair_flags[me] == 1

    def finish(mask):
        route = []
        for low in range(half):
            if mask >> (low % groups) & 1:
                route += [(low, low + half), (low + half, low)]

        def move(block):
            if not route:
                return block
            theirs = lax.ppermute(block, "expert", route)
            return jnp.where(flagged, theirs, block)

        def run(rows, grads, dpre, hidden, recv_in, recv_out, back, pick, gates):
            own_in = lax.dot_general(rows, dpre[:, :quarter], first, preferred_element_type=F32)
            own_in = move((own_in + recv_in.astype(F32)).astype(BF16))
            own_out = lax.dot_general(hidden[:, :quarter], grads, first, preferred_element_type=F32)
            own_out = move((own_out + recv_out.astype(F32)).astype(BF16))
            picked = lax.dot_general(pick, back.reshape(slots, width), first,
                                     preferred_element_type=F32)
            weighted = gates.reshape(local_tokens, top, 1) * picked.reshape(local_tokens, top, width)
            return jnp.sum(weighted, axis=1).astype(BF16), own_in, own_out

        return run

    mixed, own_in, own_out = lax.switch(
        which, [finish(mask) for mask in range(1 << groups)],
        rows, grads, dpre, hidden, recv_in, recv_out, back, pick, gates,
    )
    return mixed, own_in[None], own_out[None]


def solution(mesh):
    placed = (
        P(("dp", "expert"), None),
        P(("dp", "expert"), None),
        P(("dp", "expert"), None),
        P(("dp", "expert"), None),
        P(),
        P("expert", None, "dp"),
        P("expert", "dp", None),
    )
    return jax.shard_map(
        body,
        mesh=mesh,
        in_specs=placed,
        out_specs=(P(("dp", "expert"), None), P("expert", None, "dp"), P("expert", "dp", None)),
        check_vma=False,
    )
```

```python
import functools

import jax
import jax.numpy as jnp
from jax import lax
from jax.experimental import pallas as pl
from jax.experimental.pallas import tpu as pltpu
from jax.sharding import PartitionSpec as P

MESH = pl.DeviceIdType.MESH
F32 = jnp.float32
BF16 = jnp.bfloat16
PIECES = 4


def remote(src, dst, send, recv, target):
    copy = pltpu.make_async_remote_copy(
        src_ref=src,
        dst_ref=dst,
        send_sem=send,
        recv_sem=recv,
        device_id=target,
        device_id_type=MESH,
    )
    copy.start()
    return copy


def places(count):
    dp, me = lax.axis_index("dp"), lax.axis_index("expert")
    sibling = (dp + 1 - 2 * lax.rem(dp, 2), me)
    across = (lax.rem(dp + 2, 4), me)
    ahead = [None] + [lax.rem(me + k, count) for k in range(1, count)]
    behind = [None] + [lax.rem(me + count - k, count) for k in range(1, count)]
    return dp, me, sibling, across, ahead, behind


def greet(dp, sibling, across, ahead):
    barrier = pltpu.get_barrier_semaphore()
    targets = [sibling, across] + [(dp, peer) for peer in ahead[1:]]
    for target in targets:
        pl.semaphore_signal(barrier, inc=1, device_id=target, device_id_type=MESH)
    pl.semaphore_wait(barrier, len(targets))


def dispatch_kernel(count, x_ref, s_ref, win_ref, wout_ref, rows, grads, win_other, wout_pair,
                    a_send, a_recv, f_send, f_recv, w_send, w_recv, local):
    dp, me, sibling, across, ahead, behind = places(count)
    greet(dp, sibling, across, ahead)
    held = [
        remote(win_ref, win_other, w_send.at[0], w_recv.at[0], across),
        remote(wout_ref, wout_pair.at[1], w_send.at[1], w_recv.at[1], across),
    ]
    own = [pltpu.make_async_copy(wout_ref, wout_pair.at[0], local.at[2])]
    sent = []
    for at, (source, landed) in enumerate(((x_ref, rows), (s_ref, grads))):
        sent.append([None] + [
            remote(source.at[ahead[k]], landed.at[0, me], a_send.at[at, k], a_recv.at[at, k],
                   (dp, ahead[k]))
            for k in range(1, count)
        ])
    for at, (source, landed) in enumerate(((x_ref, rows), (s_ref, grads))):
        own.append(pltpu.make_async_copy(source.at[me], landed.at[0, me], local.at[at]))
        held.append(
            remote(source.at[me], landed.at[1, me], f_send.at[at, 0], f_recv.at[at, 0], sibling)
        )
    for copy in own:
        copy.start()
    for at, landed in enumerate((rows, grads)):
        for k in range(1, count):
            sent[at][k].wait_recv()
            block = behind[k]
            held.append(
                remote(landed.at[0, block], landed.at[1, block], f_send.at[at, k],
                       f_recv.at[at, k], sibling)
            )
    for copy in own:
        copy.wait()
    for group in sent:
        for copy in group[1:]:
            copy.wait_send()
    for copy in held:
        copy.wait()


def dispatch(x_send, s_send, win, wout, count):
    blocks = (2,) + x_send.shape
    anywhere = pl.BlockSpec(memory_space=pl.ANY)
    dma = pltpu.SemaphoreType.DMA
    return pl.pallas_call(
        functools.partial(dispatch_kernel, count),
        out_shape=(
            jax.ShapeDtypeStruct(blocks, BF16),
            jax.ShapeDtypeStruct(blocks, BF16),
            jax.ShapeDtypeStruct(win.shape, BF16),
            jax.ShapeDtypeStruct((2,) + wout.shape, BF16),
        ),
        in_specs=[anywhere] * 4,
        out_specs=(anywhere,) * 4,
        scratch_shapes=[
            dma((2, count)), dma((2, count)), dma((2, count)), dma((2, count)),
            dma((2,)), dma((2,)), dma((3,)),
        ],
        compiler_params=pltpu.CompilerParams(collective_id=0, has_side_effects=True),
    )(x_send, s_send, win, wout)


def combine_kernel(count, plan, part_ref, sin_ref, sout_ref, kin_ref, kout_ref,
                   back, own_in, own_out, their_in, their_out,
                   mine, theirs, total, held_in, held_out, got_in, got_out,
                   first_in, first_out, second_in, second_out,
                   p_send, p_recv, x_send, x_recv, r_send, r_recv, local,
                   load, store, z_send, z_recv, h_send, h_recv):
    dp, me, sibling, across, ahead, behind = places(count)
    greet(dp, sibling, across, ahead)
    groups, direct, detour = plan
    group = lax.rem(me, groups)
    beside = me + 1 - 2 * lax.rem(me, 2)
    beside_group = lax.rem(beside, groups)
    partner = lax.rem(me + count // 2, count)

    def when(value, members, act):
        if members:
            named = value == members[0]
            for member in members[1:]:
                named = jnp.logical_or(named, value == member)
            pl.when(named)(act)

    chunks = []
    for piece in range(PIECES):
        for sent_ref, kept_ref, held, got, first, second, own, their in (
            (sin_ref, kin_ref, held_in, got_in, first_in, second_in, own_in, their_in),
            (sout_ref, kout_ref, held_out, got_out, first_out, second_out, own_out, their_out),
        ):
            rows = sent_ref.shape[0] // PIECES
            cut = pl.ds(piece * rows, rows)
            chunks.append([ref.at[cut] for ref in
                           (sent_ref, kept_ref, held, got, first, second, own, their)])

    order = ahead[1:] + [me]
    parts, own, shares, loads = [], [], [], []
    for at, block in enumerate(order):
        parts.append(
            remote(part_ref.at[1, block], theirs.at[block], p_send.at[at], p_recv.at[at], sibling)
        )
        own.append(pltpu.make_async_copy(part_ref.at[0, block], mine.at[block], local.at[at]))
        own[-1].start()
    for c, (sent_ref, kept_ref, held, got, _, _, _, _) in enumerate(chunks):
        shares.append(remote(sent_ref, got, x_send.at[c], x_recv.at[c], across))
        loads.append(pltpu.make_async_copy(kept_ref, held, load.at[c]))
        loads[-1].start()
    sent = []
    for at, block in enumerate(order):
        own[at].wait()
        parts[at].wait_recv()
        total[block] = (mine[block].astype(F32) + theirs[block].astype(F32)).astype(BF16)
        if at < count - 1:
            sent.append(
                remote(total.at[block], back.at[me], r_send.at[at], r_recv.at[at], (dp, block))
            )
        else:
            last = pltpu.make_async_copy(total.at[block], back.at[me], local.at[count])
            last.start()

    def copy(src, dst, c, hop, target):
        sends, recvs = (z_send.at[c], z_recv.at[c]) if hop == 0 else (
            h_send.at[hop - 1, c], h_recv.at[hop - 1, c])
        return pltpu.make_async_remote_copy(
            src_ref=src, dst_ref=dst, send_sem=sends, recv_sem=recvs, device_id=(dp, target),
            device_id_type=MESH,
        )

    straight, hops, stores = [], [], []
    for c, (_, _, held, got, first, second, kept, their) in enumerate(chunks):
        straight.append(copy(held, their, c, 0, partner))
        hops.append((copy(held, first, c, 1, beside), copy(first, second, c, 2, partner),
                     copy(second, their, c, 3, beside)))
        stores.append(pltpu.make_async_copy(held, kept, store.at[c]))

    def relay(c, hop):
        def act():
            hops[c][hop - 1].wait_recv()
            hops[c][hop].start()
        when(beside_group, detour[c], act)

    for c, (_, _, held, got, _, _, _, _) in enumerate(chunks):
        loads[c].wait()
        shares[c].wait_recv()
        held[...] = (held[...].astype(F32) + got[...].astype(F32)).astype(BF16)
        stores[c].start()
        when(group, direct[c], straight[c].start)
        when(group, detour[c], hops[c][0].start)
        if c >= 1:
            relay(c - 1, 1)
        if c >= 2:
            relay(c - 2, 2)
    relay(len(chunks) - 1, 1)
    relay(len(chunks) - 2, 2)
    relay(len(chunks) - 1, 2)

    last.wait()
    for item in parts + shares:
        item.wait_send()
    for item in sent:
        item.wait()
    for c in range(len(chunks)):
        stores[c].wait()
        when(group, direct[c], straight[c].wait)
        when(beside_group, detour[c], hops[c][1].wait_send)
        when(beside_group, detour[c], hops[c][2].wait_send)
        when(group, detour[c], hops[c][0].wait_send)
        when(group, detour[c], hops[c][2].wait_recv)


def combine(part, sin, sout, kin, kout, count, plan, number):
    blocks = part.shape[1:]
    anywhere = pl.BlockSpec(memory_space=pl.ANY)
    dma = pltpu.SemaphoreType.DMA
    shape_in, shape_out = (jax.ShapeDtypeStruct(a.shape, BF16) for a in (sin, sout))
    pair = [pltpu.VMEM(sin.shape, BF16), pltpu.VMEM(sout.shape, BF16)]
    total = 2 * PIECES
    return pl.pallas_call(
        functools.partial(combine_kernel, count, plan),
        out_shape=(
            jax.ShapeDtypeStruct(blocks, BF16), shape_in, shape_out, shape_in, shape_out,
        ),
        in_specs=[anywhere] * 5,
        out_specs=(anywhere,) * 5,
        scratch_shapes=[pltpu.VMEM(blocks, BF16)] * 3 + pair * 4 + [
            dma((count,)), dma((count,)), dma((total,)), dma((total,)),
            dma((count,)), dma((count,)), dma((count + 1,)),
            dma((total,)), dma((total,)), dma((total,)), dma((total,)),
            dma((3, total)), dma((3, total)),
        ],
        compiler_params=pltpu.CompilerParams(
            collective_id=1 + number, has_side_effects=True, vmem_limit_bytes=48 * 1024 * 1024
        ),
    )(part, sin, sout, kin, kout)


def relocation_plan(mask, groups):
    total = 2 * PIECES
    active = [g for g in range(groups) if mask >> g & 1]
    direct, detour = [[] for _ in range(total)], [[] for _ in range(total)]
    for g in active:
        here = sum(1 for other in active if other % 2 == g % 2)
        spare = max(0, here - (len(active) - here)) if groups > 1 else 0
        round_count = total * spare // (2 * here)
        chosen = set((0, 2, 3, 5)[:round_count] if round_count > 2 else (0, 3)[:round_count])
        for c in range(total):
            (detour if c in chosen else direct)[c].append(g)
    return groups, direct, detour


def body(tokens, cotangent, expert_ids, gates, pair_flags, w_in, w_out):
    count = lax.axis_size("expert")
    me = lax.axis_index("expert")
    half = count // 2
    local_tokens, top = expert_ids.shape
    width = tokens.shape[1]
    routes = local_tokens * top
    capacity = -(-max(2, 3 * routes // (2 * count)) // 16) * 16
    slots = count * capacity
    quarter_in, quarter_out = w_in[0], w_out[0]
    quarter = quarter_in.shape[1]
    last = (((1,), (1,)), ((), ()))
    first = (((0,), (0,)), ((), ()))

    ids = expert_ids.reshape(-1)
    onehot = ids[:, None] == jnp.arange(count, dtype=jnp.int32)[None, :]
    at = jnp.arange(routes, dtype=jnp.int32)
    before = (at[None, :] < at[:, None]).astype(BF16)
    rank = jnp.dot(before, onehot.astype(BF16), preferred_element_type=F32)
    position = jnp.sum(jnp.where(onehot, rank, 0.0), axis=1).astype(jnp.int32)
    slot_of = ids * capacity + position
    pick = (jnp.arange(slots, dtype=jnp.int32)[:, None] == slot_of[None, :]).astype(BF16)
    scaled = (gates.reshape(local_tokens, top, 1) * cotangent[:, None, :].astype(F32)).astype(BF16)
    scaled = scaled.reshape(routes, width)
    copied = tokens if top == 1 else jnp.repeat(tokens, top, axis=0)
    x_send = jnp.dot(pick, copied, preferred_element_type=F32).astype(BF16)
    s_send = jnp.dot(pick, scaled, preferred_element_type=F32).astype(BF16)

    rows, grads, other_in, pair_out = dispatch(
        x_send.reshape(count, capacity, width), s_send.reshape(count, capacity, width),
        quarter_in, quarter_out, count,
    )
    rows, grads = rows.reshape(2 * slots, width), grads.reshape(2 * slots, width)
    both_out = pair_out.reshape(2 * quarter, width)
    pre = jnp.concatenate(
        [jnp.dot(rows, quarter_in, preferred_element_type=F32),
         jnp.dot(rows, other_in, preferred_element_type=F32)], axis=1)
    sig = jax.nn.sigmoid(pre)
    hidden = (pre * sig).astype(BF16)
    part = jnp.dot(hidden, both_out, preferred_element_type=F32).astype(BF16)
    dhid = lax.dot_general(grads, both_out, last, preferred_element_type=F32)
    dpre = (dhid * sig * (1.0 + pre * (1.0 - sig))).astype(BF16)
    grad_in = [
        lax.dot_general(rows, share, first, preferred_element_type=F32).astype(BF16)
        for share in (dpre[:, :quarter], dpre[:, quarter:])
    ]
    grad_out = [
        lax.dot_general(share, grads, first, preferred_element_type=F32).astype(BF16)
        for share in (hidden[:, :quarter], hidden[:, quarter:])
    ]

    groups = 4 if half == 4 else 1
    chosen = pair_flags[:half].reshape(half // groups, groups).max(axis=0)
    which = jnp.sum(chosen << jnp.arange(groups, dtype=jnp.int32))

    def branch(mask):
        plan = relocation_plan(mask, groups)
        return lambda *operands: combine(*operands, count, plan, mask)

    back, own_in, own_out, their_in, their_out = lax.switch(
        which, [branch(mask) for mask in range(1 << groups)],
        part.reshape(2, count, capacity, width), grad_in[1], grad_out[1], grad_in[0], grad_out[0],
    )
    flagged = pair_flags[me] == 1
    picked = lax.dot_general(pick, back.reshape(slots, width), first, preferred_element_type=F32)
    weighted = gates.reshape(local_tokens, top, 1) * picked.reshape(local_tokens, top, width)
    mixed = jnp.sum(weighted, axis=1).astype(BF16)
    own_in = jnp.where(flagged, their_in, own_in)
    own_out = jnp.where(flagged, their_out, own_out)
    return mixed, own_in[None], own_out[None]


def solution(mesh):
    placed = (
        P(("dp", "expert"), None),
        P(("dp", "expert"), None),
        P(("dp", "expert"), None),
        P(("dp", "expert"), None),
        P(),
        P("expert", None, "dp"),
        P("expert", "dp", None),
    )
    return jax.shard_map(
        body,
        mesh=mesh,
        in_specs=placed,
        out_specs=(P(("dp", "expert"), None), P("expert", None, "dp"), P("expert", "dp", None)),
        check_vma=False,
    )
```

```python
import functools

import jax
import jax.numpy as jnp
from jax import lax
from jax.experimental import pallas as pl
from jax.experimental.pallas import tpu as pltpu
from jax.sharding import PartitionSpec as P

MESH = pl.DeviceIdType.MESH
F32 = jnp.float32
BF16 = jnp.bfloat16
PIECES = 4
FLIGHT = 2


def remote(src, dst, send, recv, target):
    copy = pltpu.make_async_remote_copy(
        src_ref=src,
        dst_ref=dst,
        send_sem=send,
        recv_sem=recv,
        device_id=target,
        device_id_type=MESH,
    )
    copy.start()
    return copy


def places(count):
    dp, me = lax.axis_index("dp"), lax.axis_index("expert")
    sibling = (dp + 1 - 2 * lax.rem(dp, 2), me)
    across = (lax.rem(dp + 2, 4), me)
    ahead = [None] + [lax.rem(me + k, count) for k in range(1, count)]
    behind = [None] + [lax.rem(me + count - k, count) for k in range(1, count)]
    return dp, me, sibling, across, ahead, behind


def greet(dp, sibling, across, ahead):
    barrier = pltpu.get_barrier_semaphore()
    targets = [sibling, across] + [(dp, peer) for peer in ahead[1:]]
    for target in targets:
        pl.semaphore_signal(barrier, inc=1, device_id=target, device_id_type=MESH)
    pl.semaphore_wait(barrier, len(targets))


def dispatch_kernel(count, x_ref, s_ref, win_ref, wout_ref, rows, grads, win_other, wout_pair,
                    a_send, a_recv, f_send, f_recv, w_send, w_recv, local):
    dp, me, sibling, across, ahead, behind = places(count)
    greet(dp, sibling, across, ahead)
    held = [
        remote(win_ref, win_other, w_send.at[0], w_recv.at[0], across),
        remote(wout_ref, wout_pair.at[1], w_send.at[1], w_recv.at[1], across),
    ]
    own = [pltpu.make_async_copy(wout_ref, wout_pair.at[0], local.at[2])]
    sent = []
    for at, (source, landed) in enumerate(((x_ref, rows), (s_ref, grads))):
        sent.append([None] + [
            remote(source.at[ahead[k]], landed.at[0, me], a_send.at[at, k], a_recv.at[at, k],
                   (dp, ahead[k]))
            for k in range(1, count)
        ])
    for at, (source, landed) in enumerate(((x_ref, rows), (s_ref, grads))):
        own.append(pltpu.make_async_copy(source.at[me], landed.at[0, me], local.at[at]))
        held.append(
            remote(source.at[me], landed.at[1, me], f_send.at[at, 0], f_recv.at[at, 0], sibling)
        )
    for copy in own:
        copy.start()
    for at, landed in enumerate((rows, grads)):
        for k in range(1, count):
            sent[at][k].wait_recv()
            block = behind[k]
            held.append(
                remote(landed.at[0, block], landed.at[1, block], f_send.at[at, k],
                       f_recv.at[at, k], sibling)
            )
    for copy in own:
        copy.wait()
    for group in sent:
        for copy in group[1:]:
            copy.wait_send()
    for copy in held:
        copy.wait()


def dispatch(x_send, s_send, win, wout, count):
    blocks = (2,) + x_send.shape
    anywhere = pl.BlockSpec(memory_space=pl.ANY)
    dma = pltpu.SemaphoreType.DMA
    return pl.pallas_call(
        functools.partial(dispatch_kernel, count),
        out_shape=(
            jax.ShapeDtypeStruct(blocks, BF16),
            jax.ShapeDtypeStruct(blocks, BF16),
            jax.ShapeDtypeStruct(win.shape, BF16),
            jax.ShapeDtypeStruct((2,) + wout.shape, BF16),
        ),
        in_specs=[anywhere] * 4,
        out_specs=(anywhere,) * 4,
        scratch_shapes=[
            dma((2, count)), dma((2, count)), dma((2, count)), dma((2, count)),
            dma((2,)), dma((2,)), dma((3,)),
        ],
        compiler_params=pltpu.CompilerParams(collective_id=0, has_side_effects=True),
    )(x_send, s_send, win, wout)


def add_rows(out, left, right):
    rows, width = out.shape
    step = 16 if width > 1024 else 128 if rows % 128 == 0 else rows

    def act(at, carry):
        cut = pl.ds(pl.multiple_of(at * step, step), step)
        out[cut] = (left[cut].astype(F32) + right[cut].astype(F32)).astype(BF16)
        return carry

    lax.fori_loop(0, rows // step, act, 0)


def combine_kernel(count, plan, part_ref, sin_ref, sout_ref, kin_ref, kout_ref,
                   back, own_in, own_out, their_in, their_out,
                   mine, theirs, total, held_in, held_out, got_in, got_out,
                   first_in, first_out, second_in, second_out,
                   p_send, p_recv, x_send, x_recv, r_send, r_recv, local,
                   load, store, z_send, z_recv, h_send, h_recv):
    dp, me, sibling, across, ahead, behind = places(count)
    greet(dp, sibling, across, ahead)
    groups, direct, detour = plan
    group = lax.rem(me, groups)
    beside = me + 1 - 2 * lax.rem(me, 2)
    beside_group = lax.rem(beside, groups)
    partner = lax.rem(me + count // 2, count)

    def when(value, members, act):
        if members:
            named = value == members[0]
            for member in members[1:]:
                named = jnp.logical_or(named, value == member)
            pl.when(named)(act)

    chunks = []
    for piece in range(PIECES):
        for sent_ref, kept_ref, held, got, first, second, own, their in (
            (sin_ref, kin_ref, held_in, got_in, first_in, second_in, own_in, their_in),
            (sout_ref, kout_ref, held_out, got_out, first_out, second_out, own_out, their_out),
        ):
            rows = sent_ref.shape[0] // PIECES
            cut = pl.ds(piece * rows, rows)
            chunks.append([ref.at[cut] for ref in
                           (sent_ref, kept_ref, held, got, first, second, own, their)])

    order = ahead[1:] + [me]
    parts, own, shares, loads = [], [], [], []
    for at, block in enumerate(order):
        parts.append(
            remote(part_ref.at[1, block], theirs.at[block], p_send.at[at], p_recv.at[at], sibling)
        )
        own.append(pltpu.make_async_copy(part_ref.at[0, block], mine.at[block], local.at[at]))
        own[-1].start()
    def share(c):
        return remote(chunks[c][0], chunks[c][3], x_send.at[c], x_recv.at[c], across)

    for c in range(FLIGHT):
        shares.append(share(c))
    for c, (sent_ref, kept_ref, held, got, _, _, _, _) in enumerate(chunks):
        loads.append(pltpu.make_async_copy(kept_ref, held, load.at[c]))
        loads[-1].start()
    sent = []

    def settle(at):
        block = order[at]
        own[at].wait()
        parts[at].wait_recv()
        add_rows(total.at[block], mine.at[block], theirs.at[block])
        if at < count - 1:
            sent.append(
                remote(total.at[block], back.at[me], r_send.at[at], r_recv.at[at], (dp, block))
            )
        else:
            sent.append(pltpu.make_async_copy(total.at[block], back.at[me], local.at[count]))
            sent[-1].start()

    def copy(src, dst, c, hop, target):
        sends, recvs = (z_send.at[c], z_recv.at[c]) if hop == 0 else (
            h_send.at[hop - 1, c], h_recv.at[hop - 1, c])
        return pltpu.make_async_remote_copy(
            src_ref=src, dst_ref=dst, send_sem=sends, recv_sem=recvs, device_id=(dp, target),
            device_id_type=MESH,
        )

    straight, hops, stores = [], [], []
    for c, (_, _, held, got, first, second, kept, their) in enumerate(chunks):
        straight.append(copy(held, their, c, 0, partner))
        hops.append((copy(held, first, c, 1, beside), copy(first, second, c, 2, partner),
                     copy(second, their, c, 3, beside)))
        stores.append(pltpu.make_async_copy(held, kept, store.at[c]))

    def relay(c, hop):
        def act():
            hops[c][hop - 1].wait_recv()
            hops[c][hop].start()
        when(beside_group, detour[c], act)

    for c, (_, _, held, got, _, _, _, _) in enumerate(chunks):
        for at in range(c * count // len(chunks), (c + 1) * count // len(chunks)):
            settle(at)
        loads[c].wait()
        shares[c].wait_recv()
        if c + FLIGHT < len(chunks):
            shares.append(share(c + FLIGHT))
        add_rows(held, held, got)
        stores[c].start()
        when(group, direct[c], straight[c].start)
        when(group, detour[c], hops[c][0].start)
        if c >= 1:
            relay(c - 1, 1)
        if c >= 2:
            relay(c - 2, 2)
    relay(len(chunks) - 1, 1)
    relay(len(chunks) - 2, 2)
    relay(len(chunks) - 1, 2)

    for item in parts + shares:
        item.wait_send()
    for item in sent:
        item.wait()
    for c in range(len(chunks)):
        stores[c].wait()
        when(group, direct[c], straight[c].wait)
        when(beside_group, detour[c], hops[c][1].wait_send)
        when(beside_group, detour[c], hops[c][2].wait_send)
        when(group, detour[c], hops[c][0].wait_send)
        when(group, detour[c], hops[c][2].wait_recv)


def combine(part, sin, sout, kin, kout, count, plan, number):
    blocks = part.shape[1:]
    anywhere = pl.BlockSpec(memory_space=pl.ANY)
    dma = pltpu.SemaphoreType.DMA
    shape_in, shape_out = (jax.ShapeDtypeStruct(a.shape, BF16) for a in (sin, sout))
    pair = [pltpu.VMEM(sin.shape, BF16), pltpu.VMEM(sout.shape, BF16)]
    total = 2 * PIECES
    return pl.pallas_call(
        functools.partial(combine_kernel, count, plan),
        out_shape=(
            jax.ShapeDtypeStruct(blocks, BF16), shape_in, shape_out, shape_in, shape_out,
        ),
        in_specs=[anywhere] * 5,
        out_specs=(anywhere,) * 5,
        scratch_shapes=[pltpu.VMEM(blocks, BF16)] * 3 + pair * 4 + [
            dma((count,)), dma((count,)), dma((total,)), dma((total,)),
            dma((count,)), dma((count,)), dma((count + 1,)),
            dma((total,)), dma((total,)), dma((total,)), dma((total,)),
            dma((3, total)), dma((3, total)),
        ],
        compiler_params=pltpu.CompilerParams(
            collective_id=1 + number, has_side_effects=True, vmem_limit_bytes=48 * 1024 * 1024
        ),
    )(part, sin, sout, kin, kout)


def relocation_plan(mask, groups):
    total = 2 * PIECES
    active = [g for g in range(groups) if mask >> g & 1]
    direct, detour = [[] for _ in range(total)], [[] for _ in range(total)]
    for g in active:
        here = sum(1 for other in active if other % 2 == g % 2)
        spare = max(0, here - (len(active) - here)) if groups > 1 else 0
        round_count = total * spare // (2 * here)
        chosen = set((0, 2, 3, 5)[:round_count] if round_count > 2 else (0, 3)[:round_count])
        for c in range(total):
            (detour if c in chosen else direct)[c].append(g)
    return groups, direct, detour


def body(tokens, cotangent, expert_ids, gates, pair_flags, w_in, w_out):
    count = lax.axis_size("expert")
    me = lax.axis_index("expert")
    half = count // 2
    local_tokens, top = expert_ids.shape
    width = tokens.shape[1]
    routes = local_tokens * top
    capacity = -(-max(2, 3 * routes // (2 * count)) // 16) * 16
    slots = count * capacity
    quarter_in, quarter_out = w_in[0], w_out[0]
    quarter = quarter_in.shape[1]
    last = (((1,), (1,)), ((), ()))
    first = (((0,), (0,)), ((), ()))

    ids = expert_ids.reshape(-1)
    onehot = ids[:, None] == jnp.arange(count, dtype=jnp.int32)[None, :]
    at = jnp.arange(routes, dtype=jnp.int32)
    before = (at[None, :] < at[:, None]).astype(BF16)
    rank = jnp.dot(before, onehot.astype(BF16), preferred_element_type=F32)
    position = jnp.sum(jnp.where(onehot, rank, 0.0), axis=1).astype(jnp.int32)
    slot_of = ids * capacity + position
    pick = (jnp.arange(slots, dtype=jnp.int32)[:, None] == slot_of[None, :]).astype(BF16)
    scaled = (gates.reshape(local_tokens, top, 1) * cotangent[:, None, :].astype(F32)).astype(BF16)
    scaled = scaled.reshape(routes, width)
    copied = tokens if top == 1 else jnp.repeat(tokens, top, axis=0)
    x_send = jnp.dot(pick, copied, preferred_element_type=F32).astype(BF16)
    s_send = jnp.dot(pick, scaled, preferred_element_type=F32).astype(BF16)

    rows, grads, other_in, pair_out = dispatch(
        x_send.reshape(count, capacity, width), s_send.reshape(count, capacity, width),
        quarter_in, quarter_out, count,
    )
    rows, grads = rows.reshape(2 * slots, width), grads.reshape(2 * slots, width)
    both_out = pair_out.reshape(2 * quarter, width)
    pre = jnp.concatenate(
        [jnp.dot(rows, quarter_in, preferred_element_type=F32),
         jnp.dot(rows, other_in, preferred_element_type=F32)], axis=1)
    sig = jax.nn.sigmoid(pre)
    hidden = (pre * sig).astype(BF16)
    part = jnp.dot(hidden, both_out, preferred_element_type=F32).astype(BF16)
    dhid = lax.dot_general(grads, both_out, last, preferred_element_type=F32)
    dpre = (dhid * sig * (1.0 + pre * (1.0 - sig))).astype(BF16)
    grad_in = [
        lax.dot_general(rows, share, first, preferred_element_type=F32).astype(BF16)
        for share in (dpre[:, :quarter], dpre[:, quarter:])
    ]
    grad_out = [
        lax.dot_general(share, grads, first, preferred_element_type=F32).astype(BF16)
        for share in (hidden[:, :quarter], hidden[:, quarter:])
    ]

    groups = 4 if half == 4 else 1
    chosen = pair_flags[:half].reshape(half // groups, groups).max(axis=0)
    which = jnp.sum(chosen << jnp.arange(groups, dtype=jnp.int32))

    def branch(mask):
        plan = relocation_plan(mask, groups)
        return lambda *operands: combine(*operands, count, plan, mask)

    back, own_in, own_out, their_in, their_out = lax.switch(
        which, [branch(mask) for mask in range(1 << groups)],
        part.reshape(2, count, capacity, width), grad_in[1], grad_out[1], grad_in[0], grad_out[0],
    )
    flagged = pair_flags[me] == 1
    picked = lax.dot_general(pick, back.reshape(slots, width), first, preferred_element_type=F32)
    weighted = gates.reshape(local_tokens, top, 1) * picked.reshape(local_tokens, top, width)
    mixed = jnp.sum(weighted, axis=1).astype(BF16)
    own_in = jnp.where(flagged, their_in, own_in)
    own_out = jnp.where(flagged, their_out, own_out)
    return mixed, own_in[None], own_out[None]


def solution(mesh):
    placed = (
        P(("dp", "expert"), None),
        P(("dp", "expert"), None),
        P(("dp", "expert"), None),
        P(("dp", "expert"), None),
        P(),
        P("expert", None, "dp"),
        P("expert", "dp", None),
    )
    return jax.shard_map(
        body,
        mesh=mesh,
        in_specs=placed,
        out_specs=(P(("dp", "expert"), None), P("expert", None, "dp"), P("expert", "dp", None)),
        check_vma=False,
    )
```

```python
import functools

import jax
import jax.numpy as jnp
from jax import lax
from jax.experimental import pallas as pl
from jax.experimental.pallas import tpu as pltpu
from jax.sharding import PartitionSpec as P

MESH = pl.DeviceIdType.MESH
F32 = jnp.float32
BF16 = jnp.bfloat16
PIECES = 4
FLIGHT = 3
LAG = 2


def remote(src, dst, send, recv, target):
    copy = pltpu.make_async_remote_copy(
        src_ref=src,
        dst_ref=dst,
        send_sem=send,
        recv_sem=recv,
        device_id=target,
        device_id_type=MESH,
    )
    copy.start()
    return copy


def places(count):
    dp, me = lax.axis_index("dp"), lax.axis_index("expert")
    sibling = (dp + 1 - 2 * lax.rem(dp, 2), me)
    across = (lax.rem(dp + 2, 4), me)
    ahead = [None] + [lax.rem(me + k, count) for k in range(1, count)]
    behind = [None] + [lax.rem(me + count - k, count) for k in range(1, count)]
    return dp, me, sibling, across, ahead, behind


def greet(dp, sibling, across, ahead):
    barrier = pltpu.get_barrier_semaphore()
    targets = [sibling, across] + [(dp, peer) for peer in ahead[1:]]
    for target in targets:
        pl.semaphore_signal(barrier, inc=1, device_id=target, device_id_type=MESH)
    pl.semaphore_wait(barrier, len(targets))


def dispatch_kernel(count, x_ref, s_ref, win_ref, wout_ref, rows, grads, win_other, wout_pair,
                    a_send, a_recv, f_send, f_recv, w_send, w_recv, local):
    dp, me, sibling, across, ahead, behind = places(count)
    greet(dp, sibling, across, ahead)
    held = [
        remote(win_ref, win_other, w_send.at[0], w_recv.at[0], across),
        remote(wout_ref, wout_pair.at[1], w_send.at[1], w_recv.at[1], across),
    ]
    own = [pltpu.make_async_copy(wout_ref, wout_pair.at[0], local.at[2])]
    sent = []
    for at, (source, landed) in enumerate(((x_ref, rows), (s_ref, grads))):
        sent.append([None] + [
            remote(source.at[ahead[k]], landed.at[0, me], a_send.at[at, k], a_recv.at[at, k],
                   (dp, ahead[k]))
            for k in range(1, count)
        ])
    for at, (source, landed) in enumerate(((x_ref, rows), (s_ref, grads))):
        own.append(pltpu.make_async_copy(source.at[me], landed.at[0, me], local.at[at]))
        held.append(
            remote(source.at[me], landed.at[1, me], f_send.at[at, 0], f_recv.at[at, 0], sibling)
        )
    for copy in own:
        copy.start()
    for at, landed in enumerate((rows, grads)):
        for k in range(1, count):
            sent[at][k].wait_recv()
            block = behind[k]
            held.append(
                remote(landed.at[0, block], landed.at[1, block], f_send.at[at, k],
                       f_recv.at[at, k], sibling)
            )
    for copy in own:
        copy.wait()
    for group in sent:
        for copy in group[1:]:
            copy.wait_send()
    for copy in held:
        copy.wait()


def dispatch(x_send, s_send, win, wout, count):
    blocks = (2,) + x_send.shape
    anywhere = pl.BlockSpec(memory_space=pl.ANY)
    dma = pltpu.SemaphoreType.DMA
    return pl.pallas_call(
        functools.partial(dispatch_kernel, count),
        out_shape=(
            jax.ShapeDtypeStruct(blocks, BF16),
            jax.ShapeDtypeStruct(blocks, BF16),
            jax.ShapeDtypeStruct(win.shape, BF16),
            jax.ShapeDtypeStruct((2,) + wout.shape, BF16),
        ),
        in_specs=[anywhere] * 4,
        out_specs=(anywhere,) * 4,
        scratch_shapes=[
            dma((2, count)), dma((2, count)), dma((2, count)), dma((2, count)),
            dma((2,)), dma((2,)), dma((3,)),
        ],
        compiler_params=pltpu.CompilerParams(collective_id=0, has_side_effects=True),
    )(x_send, s_send, win, wout)


def add_rows(out, left, right):
    rows, width = out.shape
    step = 16 if width > 1024 else 128 if rows % 128 == 0 else rows

    def act(at, carry):
        cut = pl.ds(pl.multiple_of(at * step, step), step)
        out[cut] = (left[cut].astype(F32) + right[cut].astype(F32)).astype(BF16)
        return carry

    lax.fori_loop(0, rows // step, act, 0)


def combine_kernel(count, plan, part_ref, sin_ref, sout_ref, kin_ref, kout_ref,
                   back, own_in, own_out, their_in, their_out,
                   mine, theirs, total, held_in, held_out, got_in, got_out,
                   first_in, first_out, second_in, second_out,
                   p_send, p_recv, x_send, x_recv, r_send, r_recv, local,
                   load, store, z_send, z_recv, h_send, h_recv):
    dp, me, sibling, across, ahead, behind = places(count)
    greet(dp, sibling, across, ahead)
    groups, direct, detour = plan
    group = lax.rem(me, groups)
    beside = me + 1 - 2 * lax.rem(me, 2)
    beside_group = lax.rem(beside, groups)
    partner = lax.rem(me + count // 2, count)

    def when(value, members, act):
        if members:
            named = value == members[0]
            for member in members[1:]:
                named = jnp.logical_or(named, value == member)
            pl.when(named)(act)

    chunks = []
    for piece in range(PIECES):
        for sent_ref, kept_ref, held, got, first, second, own, their in (
            (sin_ref, kin_ref, held_in, got_in, first_in, second_in, own_in, their_in),
            (sout_ref, kout_ref, held_out, got_out, first_out, second_out, own_out, their_out),
        ):
            rows = sent_ref.shape[0] // PIECES
            cut = pl.ds(piece * rows, rows)
            chunks.append([ref.at[cut] for ref in
                           (sent_ref, kept_ref, held, got, first, second, own, their)])

    order = ahead[1:] + [me]
    parts, own, shares, loads = [], [], [], []
    for at, block in enumerate(order):
        parts.append(
            remote(part_ref.at[1, block], theirs.at[block], p_send.at[at], p_recv.at[at], sibling)
        )
        own.append(pltpu.make_async_copy(part_ref.at[0, block], mine.at[block], local.at[at]))
        own[-1].start()
    def share(c):
        return remote(chunks[c][0], chunks[c][3], x_send.at[c], x_recv.at[c], across)

    for c in range(FLIGHT):
        shares.append(share(c))
    for c, (sent_ref, kept_ref, held, got, _, _, _, _) in enumerate(chunks):
        loads.append(pltpu.make_async_copy(kept_ref, held, load.at[c]))
        loads[-1].start()
    sent = []

    def settle(at):
        block = order[at]
        own[at].wait()
        parts[at].wait_recv()
        add_rows(total.at[block], mine.at[block], theirs.at[block])
        if at < count - 1:
            sent.append(
                remote(total.at[block], back.at[me], r_send.at[at], r_recv.at[at], (dp, block))
            )
        else:
            sent.append(pltpu.make_async_copy(total.at[block], back.at[me], local.at[count]))
            sent[-1].start()

    def copy(src, dst, c, hop, target):
        sends, recvs = (z_send.at[c], z_recv.at[c]) if hop == 0 else (
            h_send.at[hop - 1, c], h_recv.at[hop - 1, c])
        return pltpu.make_async_remote_copy(
            src_ref=src, dst_ref=dst, send_sem=sends, recv_sem=recvs, device_id=(dp, target),
            device_id_type=MESH,
        )

    straight, hops, stores = [], [], []
    for c, (_, _, held, got, first, second, kept, their) in enumerate(chunks):
        straight.append(copy(held, their, c, 0, partner))
        hops.append((copy(held, first, c, 1, beside), copy(first, second, c, 2, partner),
                     copy(second, their, c, 3, beside)))
        stores.append(pltpu.make_async_copy(held, kept, store.at[c]))

    def relay(c, hop):
        def act():
            hops[c][hop - 1].wait_recv()
            hops[c][hop].start()
        when(beside_group, detour[c], act)

    for at in range(count):
        settle(at)
    for c, (_, _, held, got, _, _, _, _) in enumerate(chunks):
        loads[c].wait()
        shares[c].wait_recv()
        if c + FLIGHT < len(chunks):
            shares.append(share(c + FLIGHT))
        add_rows(held, held, got)
        stores[c].start()
        when(group, direct[c], straight[c].start)
        when(group, detour[c], hops[c][0].start)
        if c >= LAG:
            relay(c - LAG, 1)
        if c >= 2 * LAG:
            relay(c - 2 * LAG, 2)
    for c in range(len(chunks) - LAG, len(chunks) + LAG):
        if c < len(chunks):
            relay(c, 1)
        relay(c - LAG, 2)

    for item in parts + shares:
        item.wait_send()
    for item in sent:
        item.wait()
    for c in range(len(chunks)):
        stores[c].wait()
        when(group, direct[c], straight[c].wait)
        when(beside_group, detour[c], hops[c][1].wait_send)
        when(beside_group, detour[c], hops[c][2].wait_send)
        when(group, detour[c], hops[c][0].wait_send)
        when(group, detour[c], hops[c][2].wait_recv)


def combine(part, sin, sout, kin, kout, count, plan, number):
    blocks = part.shape[1:]
    anywhere = pl.BlockSpec(memory_space=pl.ANY)
    dma = pltpu.SemaphoreType.DMA
    shape_in, shape_out = (jax.ShapeDtypeStruct(a.shape, BF16) for a in (sin, sout))
    pair = [pltpu.VMEM(sin.shape, BF16), pltpu.VMEM(sout.shape, BF16)]
    total = 2 * PIECES
    return pl.pallas_call(
        functools.partial(combine_kernel, count, plan),
        out_shape=(
            jax.ShapeDtypeStruct(blocks, BF16), shape_in, shape_out, shape_in, shape_out,
        ),
        in_specs=[anywhere] * 5,
        out_specs=(anywhere,) * 5,
        scratch_shapes=[pltpu.VMEM(blocks, BF16)] * 3 + pair * 4 + [
            dma((count,)), dma((count,)), dma((total,)), dma((total,)),
            dma((count,)), dma((count,)), dma((count + 1,)),
            dma((total,)), dma((total,)), dma((total,)), dma((total,)),
            dma((3, total)), dma((3, total)),
        ],
        compiler_params=pltpu.CompilerParams(
            collective_id=1 + number, has_side_effects=True, vmem_limit_bytes=48 * 1024 * 1024
        ),
    )(part, sin, sout, kin, kout)


def relocation_plan(mask, groups):
    total = 2 * PIECES
    active = [g for g in range(groups) if mask >> g & 1]
    direct, detour = [[] for _ in range(total)], [[] for _ in range(total)]
    for g in active:
        here = sum(1 for other in active if other % 2 == g % 2)
        spare = max(0, here - (len(active) - here)) if groups > 1 else 0
        round_count = total * spare // (2 * here)
        chosen = set(range(round_count))
        for c in range(total):
            (detour if c in chosen else direct)[c].append(g)
    return groups, direct, detour


def body(tokens, cotangent, expert_ids, gates, pair_flags, w_in, w_out):
    count = lax.axis_size("expert")
    me = lax.axis_index("expert")
    half = count // 2
    local_tokens, top = expert_ids.shape
    width = tokens.shape[1]
    routes = local_tokens * top
    capacity = -(-max(2, 3 * routes // (2 * count)) // 16) * 16
    slots = count * capacity
    quarter_in, quarter_out = w_in[0], w_out[0]
    quarter = quarter_in.shape[1]
    last = (((1,), (1,)), ((), ()))
    first = (((0,), (0,)), ((), ()))

    ids = expert_ids.reshape(-1)
    onehot = ids[:, None] == jnp.arange(count, dtype=jnp.int32)[None, :]
    at = jnp.arange(routes, dtype=jnp.int32)
    before = (at[None, :] < at[:, None]).astype(BF16)
    rank = jnp.dot(before, onehot.astype(BF16), preferred_element_type=F32)
    position = jnp.sum(jnp.where(onehot, rank, 0.0), axis=1).astype(jnp.int32)
    slot_of = ids * capacity + position
    pick = (jnp.arange(slots, dtype=jnp.int32)[:, None] == slot_of[None, :]).astype(BF16)
    scaled = (gates.reshape(local_tokens, top, 1) * cotangent[:, None, :].astype(F32)).astype(BF16)
    scaled = scaled.reshape(routes, width)
    copied = tokens if top == 1 else jnp.repeat(tokens, top, axis=0)
    x_send = jnp.dot(pick, copied, preferred_element_type=F32).astype(BF16)
    s_send = jnp.dot(pick, scaled, preferred_element_type=F32).astype(BF16)

    rows, grads, other_in, pair_out = dispatch(
        x_send.reshape(count, capacity, width), s_send.reshape(count, capacity, width),
        quarter_in, quarter_out, count,
    )
    rows, grads = rows.reshape(2 * slots, width), grads.reshape(2 * slots, width)
    both_out = pair_out.reshape(2 * quarter, width)
    pre = jnp.concatenate(
        [jnp.dot(rows, quarter_in, preferred_element_type=F32),
         jnp.dot(rows, other_in, preferred_element_type=F32)], axis=1)
    sig = jax.nn.sigmoid(pre)
    hidden = (pre * sig).astype(BF16)
    part = jnp.dot(hidden, both_out, preferred_element_type=F32).astype(BF16)
    dhid = lax.dot_general(grads, both_out, last, preferred_element_type=F32)
    dpre = (dhid * sig * (1.0 + pre * (1.0 - sig))).astype(BF16)
    grad_in = [
        lax.dot_general(rows, share, first, preferred_element_type=F32).astype(BF16)
        for share in (dpre[:, :quarter], dpre[:, quarter:])
    ]
    grad_out = [
        lax.dot_general(share, grads, first, preferred_element_type=F32).astype(BF16)
        for share in (hidden[:, :quarter], hidden[:, quarter:])
    ]

    groups = 4 if half == 4 else 1
    chosen = pair_flags[:half].reshape(half // groups, groups).max(axis=0)
    which = jnp.sum(chosen << jnp.arange(groups, dtype=jnp.int32))

    def branch(mask):
        plan = relocation_plan(mask, groups)
        return lambda *operands: combine(*operands, count, plan, mask)

    back, own_in, own_out, their_in, their_out = lax.switch(
        which, [branch(mask) for mask in range(1 << groups)],
        part.reshape(2, count, capacity, width), grad_in[1], grad_out[1], grad_in[0], grad_out[0],
    )
    flagged = pair_flags[me] == 1
    picked = lax.dot_general(pick, back.reshape(slots, width), first, preferred_element_type=F32)
    weighted = gates.reshape(local_tokens, top, 1) * picked.reshape(local_tokens, top, width)
    mixed = jnp.sum(weighted, axis=1).astype(BF16)
    own_in = jnp.where(flagged, their_in, own_in)
    own_out = jnp.where(flagged, their_out, own_out)
    return mixed, own_in[None], own_out[None]


def solution(mesh):
    placed = (
        P(("dp", "expert"), None),
        P(("dp", "expert"), None),
        P(("dp", "expert"), None),
        P(("dp", "expert"), None),
        P(),
        P("expert", None, "dp"),
        P("expert", "dp", None),
    )
    return jax.shard_map(
        body,
        mesh=mesh,
        in_specs=placed,
        out_specs=(P(("dp", "expert"), None), P("expert", None, "dp"), P("expert", "dp", None)),
        check_vma=False,
    )
```

```python
import functools

import jax
import jax.numpy as jnp
from jax import lax
from jax.experimental import pallas as pl
from jax.experimental.pallas import tpu as pltpu
from jax.sharding import PartitionSpec as P

MESH = pl.DeviceIdType.MESH
F32 = jnp.float32
BF16 = jnp.bfloat16
PIECES = 4
FLIGHT = 3
LAG = 2


def remote(src, dst, send, recv, target):
    copy = pltpu.make_async_remote_copy(
        src_ref=src,
        dst_ref=dst,
        send_sem=send,
        recv_sem=recv,
        device_id=target,
        device_id_type=MESH,
    )
    copy.start()
    return copy


def places(count):
    dp, me = lax.axis_index("dp"), lax.axis_index("expert")
    sibling = (dp + 1 - 2 * lax.rem(dp, 2), me)
    across = (lax.rem(dp + 2, 4), me)
    ahead = [None] + [lax.rem(me + k, count) for k in range(1, count)]
    behind = [None] + [lax.rem(me + count - k, count) for k in range(1, count)]
    return dp, me, sibling, across, ahead, behind


def greet(dp, sibling, across, ahead):
    barrier = pltpu.get_barrier_semaphore()
    targets = [sibling, across] + [(dp, peer) for peer in ahead[1:]]
    for target in targets:
        pl.semaphore_signal(barrier, inc=1, device_id=target, device_id_type=MESH)
    pl.semaphore_wait(barrier, len(targets))


def dispatch_kernel(count, x_ref, s_ref, win_ref, wout_ref, rows, grads, win_other, wout_pair,
                    a_send, a_recv, f_send, f_recv, w_send, w_recv, local):
    dp, me, sibling, across, ahead, behind = places(count)
    greet(dp, sibling, across, ahead)
    held = [
        remote(win_ref, win_other, w_send.at[0], w_recv.at[0], across),
        remote(wout_ref, wout_pair.at[1], w_send.at[1], w_recv.at[1], across),
    ]
    own = [pltpu.make_async_copy(wout_ref, wout_pair.at[0], local.at[2])]
    sent = []
    for at, (source, landed) in enumerate(((x_ref, rows), (s_ref, grads))):
        sent.append([None] + [
            remote(source.at[ahead[k]], landed.at[0, me], a_send.at[at, k], a_recv.at[at, k],
                   (dp, ahead[k]))
            for k in range(1, count)
        ])
    for at, (source, landed) in enumerate(((x_ref, rows), (s_ref, grads))):
        own.append(pltpu.make_async_copy(source.at[me], landed.at[0, me], local.at[at]))
        held.append(
            remote(source.at[me], landed.at[1, me], f_send.at[at, 0], f_recv.at[at, 0], sibling)
        )
    for copy in own:
        copy.start()
    for at, landed in enumerate((rows, grads)):
        for k in range(1, count):
            sent[at][k].wait_recv()
            block = behind[k]
            held.append(
                remote(landed.at[0, block], landed.at[1, block], f_send.at[at, k],
                       f_recv.at[at, k], sibling)
            )
    for copy in own:
        copy.wait()
    for group in sent:
        for copy in group[1:]:
            copy.wait_send()
    for copy in held:
        copy.wait()


def dispatch(x_send, s_send, win, wout, count):
    blocks = (2,) + x_send.shape
    anywhere = pl.BlockSpec(memory_space=pl.ANY)
    dma = pltpu.SemaphoreType.DMA
    return pl.pallas_call(
        functools.partial(dispatch_kernel, count),
        out_shape=(
            jax.ShapeDtypeStruct(blocks, BF16),
            jax.ShapeDtypeStruct(blocks, BF16),
            jax.ShapeDtypeStruct(win.shape, BF16),
            jax.ShapeDtypeStruct((2,) + wout.shape, BF16),
        ),
        in_specs=[anywhere] * 4,
        out_specs=(anywhere,) * 4,
        scratch_shapes=[
            dma((2, count)), dma((2, count)), dma((2, count)), dma((2, count)),
            dma((2,)), dma((2,)), dma((3,)),
        ],
        compiler_params=pltpu.CompilerParams(collective_id=0, has_side_effects=True),
    )(x_send, s_send, win, wout)


def add_rows(out, left, right):
    rows, width = out.shape
    high = 16 if width > 512 else 64
    wide = 512 if width % 512 == 0 else width
    across = width // wide

    def act(at, carry):
        cut = (pl.ds(pl.multiple_of((at // across) * high, high), high),
               pl.ds(pl.multiple_of(lax.rem(at, across) * wide, wide), wide))
        out[cut] = (left[cut].astype(F32) + right[cut].astype(F32)).astype(BF16)
        return carry

    lax.fori_loop(0, (rows // high) * across, act, 0)


def combine_kernel(count, plan, part_ref, sin_ref, sout_ref, kin_ref, kout_ref,
                   back, own_in, own_out, their_in, their_out,
                   mine, theirs, total, held_in, held_out, got_in, got_out,
                   first_in, first_out, second_in, second_out,
                   p_send, p_recv, x_send, x_recv, r_send, r_recv, local,
                   load, store, z_send, z_recv, h_send, h_recv):
    dp, me, sibling, across, ahead, behind = places(count)
    greet(dp, sibling, across, ahead)
    groups, direct, detour = plan
    group = lax.rem(me, groups)
    beside = me + 1 - 2 * lax.rem(me, 2)
    beside_group = lax.rem(beside, groups)
    partner = lax.rem(me + count // 2, count)

    def when(value, members, act):
        if members:
            named = value == members[0]
            for member in members[1:]:
                named = jnp.logical_or(named, value == member)
            pl.when(named)(act)

    chunks = []
    for piece in range(PIECES):
        for sent_ref, kept_ref, held, got, first, second, own, their in (
            (sin_ref, kin_ref, held_in, got_in, first_in, second_in, own_in, their_in),
            (sout_ref, kout_ref, held_out, got_out, first_out, second_out, own_out, their_out),
        ):
            rows = sent_ref.shape[0] // PIECES
            cut = pl.ds(piece * rows, rows)
            chunks.append([ref.at[cut] for ref in
                           (sent_ref, kept_ref, held, got, first, second, own, their)])

    order = ahead[1:] + [me]
    parts, own, shares, loads = [], [], [], []
    for at, block in enumerate(order):
        parts.append(
            remote(part_ref.at[1, block], theirs.at[block], p_send.at[at], p_recv.at[at], sibling)
        )
        own.append(pltpu.make_async_copy(part_ref.at[0, block], mine.at[block], local.at[at]))
        own[-1].start()
    def share(c):
        return remote(chunks[c][0], chunks[c][3], x_send.at[c], x_recv.at[c], across)

    for c in range(FLIGHT):
        shares.append(share(c))
    for c, (sent_ref, kept_ref, held, got, _, _, _, _) in enumerate(chunks):
        loads.append(pltpu.make_async_copy(kept_ref, held, load.at[c]))
        loads[-1].start()
    sent = []

    def settle(at):
        block = order[at]
        own[at].wait()
        parts[at].wait_recv()
        add_rows(total.at[block], mine.at[block], theirs.at[block])
        if at < count - 1:
            sent.append(
                remote(total.at[block], back.at[me], r_send.at[at], r_recv.at[at], (dp, block))
            )
        else:
            sent.append(pltpu.make_async_copy(total.at[block], back.at[me], local.at[count]))
            sent[-1].start()

    def copy(src, dst, c, hop, target):
        sends, recvs = (z_send.at[c], z_recv.at[c]) if hop == 0 else (
            h_send.at[hop - 1, c], h_recv.at[hop - 1, c])
        return pltpu.make_async_remote_copy(
            src_ref=src, dst_ref=dst, send_sem=sends, recv_sem=recvs, device_id=(dp, target),
            device_id_type=MESH,
        )

    straight, hops, stores = [], [], []
    for c, (_, _, held, got, first, second, kept, their) in enumerate(chunks):
        straight.append(copy(held, their, c, 0, partner))
        hops.append((copy(held, first, c, 1, beside), copy(first, second, c, 2, partner),
                     copy(second, their, c, 3, beside)))
        stores.append(pltpu.make_async_copy(held, kept, store.at[c]))

    def relay(c, hop):
        def act():
            hops[c][hop - 1].wait_recv()
            hops[c][hop].start()
        when(beside_group, detour[c], act)

    for at in range(count):
        settle(at)
    for c, (_, _, held, got, _, _, _, _) in enumerate(chunks):
        loads[c].wait()
        shares[c].wait_recv()
        if c + FLIGHT < len(chunks):
            shares.append(share(c + FLIGHT))
        add_rows(held, held, got)
        stores[c].start()
        when(group, direct[c], straight[c].start)
        when(group, detour[c], hops[c][0].start)
        if c >= LAG:
            relay(c - LAG, 1)
        if c >= 2 * LAG:
            relay(c - 2 * LAG, 2)
    for c in range(len(chunks) - LAG, len(chunks) + LAG):
        if c < len(chunks):
            relay(c, 1)
        relay(c - LAG, 2)

    for item in parts + shares:
        item.wait_send()
    for item in sent:
        item.wait()
    for c in range(len(chunks)):
        stores[c].wait()
        when(group, direct[c], straight[c].wait)
        when(beside_group, detour[c], hops[c][1].wait_send)
        when(beside_group, detour[c], hops[c][2].wait_send)
        when(group, detour[c], hops[c][0].wait_send)
        when(group, detour[c], hops[c][2].wait_recv)


def combine(part, sin, sout, kin, kout, count, plan, number):
    blocks = part.shape[1:]
    anywhere = pl.BlockSpec(memory_space=pl.ANY)
    dma = pltpu.SemaphoreType.DMA
    shape_in, shape_out = (jax.ShapeDtypeStruct(a.shape, BF16) for a in (sin, sout))
    pair = [pltpu.VMEM(sin.shape, BF16), pltpu.VMEM(sout.shape, BF16)]
    total = 2 * PIECES
    return pl.pallas_call(
        functools.partial(combine_kernel, count, plan),
        out_shape=(
            jax.ShapeDtypeStruct(blocks, BF16), shape_in, shape_out, shape_in, shape_out,
        ),
        in_specs=[anywhere] * 5,
        out_specs=(anywhere,) * 5,
        scratch_shapes=[pltpu.VMEM(blocks, BF16)] * 3 + pair * 4 + [
            dma((count,)), dma((count,)), dma((total,)), dma((total,)),
            dma((count,)), dma((count,)), dma((count + 1,)),
            dma((total,)), dma((total,)), dma((total,)), dma((total,)),
            dma((3, total)), dma((3, total)),
        ],
        compiler_params=pltpu.CompilerParams(
            collective_id=1 + number, has_side_effects=True, vmem_limit_bytes=48 * 1024 * 1024
        ),
    )(part, sin, sout, kin, kout)


def relocation_plan(mask, groups):
    total = 2 * PIECES
    active = [g for g in range(groups) if mask >> g & 1]
    direct, detour = [[] for _ in range(total)], [[] for _ in range(total)]
    for g in active:
        here = sum(1 for other in active if other % 2 == g % 2)
        spare = max(0, here - (len(active) - here)) if groups > 1 else 0
        round_count = max(0, total * spare // (2 * here) - 1)
        chosen = set(range(round_count))
        for c in range(total):
            (detour if c in chosen else direct)[c].append(g)
    return groups, direct, detour


def body(tokens, cotangent, expert_ids, gates, pair_flags, w_in, w_out):
    count = lax.axis_size("expert")
    me = lax.axis_index("expert")
    half = count // 2
    local_tokens, top = expert_ids.shape
    width = tokens.shape[1]
    routes = local_tokens * top
    capacity = -(-max(2, 3 * routes // (2 * count)) // 16) * 16
    slots = count * capacity
    quarter_in, quarter_out = w_in[0], w_out[0]
    quarter = quarter_in.shape[1]
    last = (((1,), (1,)), ((), ()))
    first = (((0,), (0,)), ((), ()))

    ids = expert_ids.reshape(-1)
    onehot = ids[:, None] == jnp.arange(count, dtype=jnp.int32)[None, :]
    at = jnp.arange(routes, dtype=jnp.int32)
    before = (at[None, :] < at[:, None]).astype(BF16)
    rank = jnp.dot(before, onehot.astype(BF16), preferred_element_type=F32)
    position = jnp.sum(jnp.where(onehot, rank, 0.0), axis=1).astype(jnp.int32)
    slot_of = ids * capacity + position
    pick = (jnp.arange(slots, dtype=jnp.int32)[:, None] == slot_of[None, :]).astype(BF16)
    scaled = (gates.reshape(local_tokens, top, 1) * cotangent[:, None, :].astype(F32)).astype(BF16)
    scaled = scaled.reshape(routes, width)
    copied = tokens if top == 1 else jnp.repeat(tokens, top, axis=0)
    x_send = jnp.dot(pick, copied, preferred_element_type=F32).astype(BF16)
    s_send = jnp.dot(pick, scaled, preferred_element_type=F32).astype(BF16)

    rows, grads, other_in, pair_out = dispatch(
        x_send.reshape(count, capacity, width), s_send.reshape(count, capacity, width),
        quarter_in, quarter_out, count,
    )
    rows, grads = rows.reshape(2 * slots, width), grads.reshape(2 * slots, width)
    both_out = pair_out.reshape(2 * quarter, width)
    pre = jnp.concatenate(
        [jnp.dot(rows, quarter_in, preferred_element_type=F32),
         jnp.dot(rows, other_in, preferred_element_type=F32)], axis=1)
    sig = jax.nn.sigmoid(pre)
    hidden = (pre * sig).astype(BF16)
    part = jnp.dot(hidden, both_out, preferred_element_type=F32).astype(BF16)
    dhid = lax.dot_general(grads, both_out, last, preferred_element_type=F32)
    dpre = (dhid * sig * (1.0 + pre * (1.0 - sig))).astype(BF16)
    grad_in = [
        lax.dot_general(rows, share, first, preferred_element_type=F32).astype(BF16)
        for share in (dpre[:, :quarter], dpre[:, quarter:])
    ]
    grad_out = [
        lax.dot_general(share, grads, first, preferred_element_type=F32).astype(BF16)
        for share in (hidden[:, :quarter], hidden[:, quarter:])
    ]

    groups = 4 if half == 4 else 1
    chosen = pair_flags[:half].reshape(half // groups, groups).max(axis=0)
    which = jnp.sum(chosen << jnp.arange(groups, dtype=jnp.int32))

    def branch(mask):
        plan = relocation_plan(mask, groups)
        return lambda *operands: combine(*operands, count, plan, mask)

    back, own_in, own_out, their_in, their_out = lax.switch(
        which, [branch(mask) for mask in range(1 << groups)],
        part.reshape(2, count, capacity, width), grad_in[1], grad_out[1], grad_in[0], grad_out[0],
    )
    flagged = pair_flags[me] == 1
    picked = lax.dot_general(pick, back.reshape(slots, width), first, preferred_element_type=F32)
    weighted = gates.reshape(local_tokens, top, 1) * picked.reshape(local_tokens, top, width)
    mixed = jnp.sum(weighted, axis=1).astype(BF16)
    own_in = jnp.where(flagged, their_in, own_in)
    own_out = jnp.where(flagged, their_out, own_out)
    return mixed, own_in[None], own_out[None]


def solution(mesh):
    placed = (
        P(("dp", "expert"), None),
        P(("dp", "expert"), None),
        P(("dp", "expert"), None),
        P(("dp", "expert"), None),
        P(),
        P("expert", None, "dp"),
        P("expert", "dp", None),
    )
    return jax.shard_map(
        body,
        mesh=mesh,
        in_specs=placed,
        out_specs=(P(("dp", "expert"), None), P("expert", None, "dp"), P("expert", "dp", None)),
        check_vma=False,
    )
```
